512 devices in a mesh: blk: 64 (over z_lo, y, core), hop: 8 (over x, z_hi).
Axes of the slice: x: 4, y: 8, z: 8 (z_hi: 2, z_lo: 4; z = z_hi * 4 + z_lo), core: 2. Of those that a mesh axis runs over, the one named last changes fastest.
Arguments:
- picture_embed_matrix: float32 [98304, 1536], P(('blk', 'hop')), may hold values from -6 to 6
- caption_embed_matrix: float32 [98304, 1536], P(('blk', 'hop')), may hold values from -6 to 6
- matching_caption_index: int32 [512, 192], P(('blk', 'hop')), may hold values from 0 to 191, each once within a row
- log_temp_param: float32 [1], replicated, may hold values from 5 to 12
- offset_shift_value: float32 [1], replicated, may hold values from -3 to 0
Outputs:
- average_line_cost: float32 [98304], P(('blk', 'hop'))
- photo_loss_slope: float32 [98304, 1536], P(('blk', 'hop'))
- words_loss_slope: float32 [98304, 1536], P(('blk', 'hop'))
The draws below stay inside these ranges and needn't reach their ends.
Inputs may be any that keep to these rules, and one draw needn't show every extreme that they name: `matching_caption_index`: each row of it is a permutation of 0 to 191.
All inputs are finite; a program needn't handle non-finite values.
Results may differ from the reference program's by a relative error of at most 0.0001.
Values sent between devices are 32-bit elements; how exact they have to be, the bound alone decides.
A program may use at most 64 MiB of HBM per device.

```python
import jax
import jax.numpy as jnp
from jax import lax

E = 1536
LINES_PER_GROUP = 192
WINDOW_OFFSETS = 2
BLOCKS = 512
TOTAL_COUPLES = 98304
COUPLES_PER_ROW = 1152
N_BLK = 64
N_HOP = 8


def block_levels(key, shape, split, low, high):
    level, own = 1.0, jax.random.fold_in(key, 6)
    for dim, parts in split:
        heights = jnp.exp(jax.random.uniform(jax.random.fold_in(own, dim), (parts,), jnp.float32, low / len(split), high / len(split)))
        level = level * jnp.repeat(heights, shape[dim] // parts).reshape([-1 if axis == dim else 1 for axis in range(len(shape))])
    return level


def normal_values(own_key, extent, width, most, split=(), kind=jnp.bfloat16):
    drawn = width * jax.random.normal(own_key, extent, jnp.float32)
    if split:
        drawn = drawn * block_levels(own_key, extent, split, -0.22, 0.18)
    return jnp.clip(drawn, -most, most).astype(kind)


def setup_inputs(seed: int = 0) -> dict:
    seeds = jax.random.split(jax.random.key(seed), 6)
    return {
        "picture_embed_matrix": normal_values(seeds[0], (TOTAL_COUPLES, E), 1.0, 6.0, ((0, 512),), jnp.float32),
        "caption_embed_matrix": normal_values(seeds[1], (TOTAL_COUPLES, E), 1.0, 6.0, ((0, 512),), jnp.float32),
        "matching_caption_index": jax.vmap(lambda own: jax.random.permutation(own, LINES_PER_GROUP))(jax.random.split(seeds[2], BLOCKS)).reshape((BLOCKS, LINES_PER_GROUP)).astype(jnp.int32),
        "log_temp_param": jnp.clip(jax.random.uniform(seeds[3], (1,), jnp.float32, 5.0, 12.0), 5.0, 12.0),
        "offset_shift_value": jnp.clip(jax.random.uniform(seeds[4], (1,), jnp.float32, -3.0, 0.0), -3.0, 0.0),
    }


def normalize(values):
    inverse = lax.rsqrt(lax.optimization_barrier(jnp.sum(values * values, axis=-1, keepdims=True)) + 1e-06)
    return (values * inverse, inverse)

def reference(picture_embed_matrix, caption_embed_matrix, matching_caption_index, log_temp_param, offset_shift_value):
    exp_logit_coef = log_temp_param[0]
    bias_added = offset_shift_value[0]
    unit_query_vec, inv_x = normalize(picture_embed_matrix)
    unit_key_vec, inv_y = normalize(caption_embed_matrix)
    query_batch = unit_query_vec.reshape(N_BLK, N_HOP, LINES_PER_GROUP, E)
    yb = unit_key_vec.reshape(N_BLK, N_HOP, LINES_PER_GROUP, E)
    column_entries = jnp.arange(LINES_PER_GROUP, dtype=jnp.int32)
    labels = (matching_caption_index.reshape(N_BLK, N_HOP, LINES_PER_GROUP)[:, :, :, None] == column_entries[None, None, None, :]).astype(jnp.float32)
    couple_losses_table = jnp.zeros((N_BLK, N_HOP, LINES_PER_GROUP), jnp.float32)
    query_partial = jnp.zeros_like(query_batch)
    gradient_wrt_target = jnp.zeros_like(yb)
    hops_done = lax.Precision.HIGHEST
    for upper in range(2):
        for step in range(WINDOW_OFFSETS + 1):
            shipped_slab = jnp.roll(yb, (step, upper), axis=(0, 1))
            cosine_score = exp_logit_coef * jnp.einsum('xawn,xaon->xawo', query_batch, shipped_slab, precision=hops_done) + bias_added
            if step == 0 and upper == 0:
                label_plus_minus = labels
            else:
                label_plus_minus = jnp.zeros_like(cosine_score)
            polarity_weighted = 2.0 * label_plus_minus - 1.0
            couple_losses_table = couple_losses_table + lax.optimization_barrier(jnp.sum(jax.nn.softplus(-polarity_weighted * cosine_score), axis=-1))
            partial_grad = jax.nn.sigmoid(cosine_score) - label_plus_minus
            query_partial = query_partial + exp_logit_coef * jnp.einsum('ptwo,ptod->ptwd', partial_grad, shipped_slab, precision=hops_done)
            part = exp_logit_coef * jnp.einsum('lqva,lqvn->lqan', partial_grad, query_batch, precision=hops_done)
            gradient_wrt_target = gradient_wrt_target + jnp.roll(part, (-step, -upper), axis=(0, 1))
    query_partial = query_partial.reshape(TOTAL_COUPLES, E)
    gradient_wrt_target = gradient_wrt_target.reshape(TOTAL_COUPLES, E)
    photo_loss_slope = inv_x * (query_partial - unit_query_vec * lax.optimization_barrier(jnp.sum(unit_query_vec * query_partial, axis=-1, keepdims=True)))
    words_loss_slope = inv_y * (gradient_wrt_target - unit_key_vec * lax.optimization_barrier(jnp.sum(unit_key_vec * gradient_wrt_target, axis=-1, keepdims=True)))
    average_line_cost = couple_losses_table.reshape(TOTAL_COUPLES) / COUPLES_PER_ROW
    return (average_line_cost, photo_loss_slope, words_loss_slope)
```

```python
import functools

import jax
import jax.numpy as jnp
from jax import lax
from jax.experimental import pallas as pl
from jax.experimental.pallas import tpu as pltpu
from jax.sharding import PartitionSpec as P

COUPLES_PER_ROW = 1152
ROWS, WIDTH = 192, 1536
CHUNKS = 4
CH = ROWS // CHUNKS
GROUP = 16
MESH = pl.DeviceIdType.MESH
F32, BF16 = jnp.float32, jnp.bfloat16
CROSS, RELAY, NEAR1, NEAR2, FAR1, FAR2 = range(6)
SLOTS = (CROSS, NEAR1, NEAR2, FAR1, FAR2)
LANES = {CROSS: 0, NEAR1: 1, NEAR2: 2, FAR1: 3, FAR2: 4}
CROSSING, NEXT, ONWARD, RELAYED, SIB_OWN, SIB_CROSS, SIB_NEAR, SIB_FAR = range(8)


def to_int(p):
    return p.astype(jnp.int32)


def pick(p, a, b):
    return tuple(jnp.where(p, u, v) for u, v in zip(a, b))


def chip(x, y, z, c):
    return ((x + 8) % 4, (y + 8) % 8, (z + 16) % 8, c)


def coordinates():
    b, h = lax.axis_index("blk"), lax.axis_index("hop")
    return h // 2, (b // 2) % 8, (h % 2) * 4 + b // 16, b % 2


def device(x, y, z, c):
    return ((z % 4) * 16 + y * 2 + c, x * 2 + z // 4)


def mirrored(place, side):
    x, y, z, c = place
    return place if side == 0 else (3 - x, 7 - y, 7 - z, 1 - c)


class Routes:
    def __init__(r, place):
        x, y, z, c = place
        zero = 0 * c
        last = y == 7
        r.lead = c == 0
        r.follow = c == 1
        r.sibling = (x, y, z, 1 - c)
        r.to_cross = chip(x + z // 4, y, z + 4, c)
        r.to_next = pick(last, chip(x, 6 - 5 * c, z + 1, c), chip(x, y + 1, z, zero))
        r.next_slot = jnp.where(last, RELAY, NEAR2 - c)
        r.to_onward = pick(
            last,
            pick(c == 0, chip(x - to_int(z == 3), zero, z + 1, c), chip(x, y, z + 1, c)),
            chip(x, y + 1, z, zero),
        )
        r.onward_slot = jnp.where(last & (c == 1), RELAY, FAR2 - c)
        r.relays_far = last & (c == 1)
        r.relays_near = ((y == 6) & (c == 0)) | ((y == 1) & (c == 1))
        r.relays = r.relays_far | r.relays_near
        r.to_relayed = chip(jnp.where(r.relays_far, x - to_int(z == 4), x + to_int(z == 0)), zero, z, zero)
        r.relayed_slot = jnp.where(r.relays_far, FAR1, NEAR2 - c)
        r.from_cross = chip(x - ((z + 4) % 8) // 4, y, z + 4, c)
        r.from_relay = chip(x, zero + 7, z - 1, c)
        near, far = x - to_int(z == 0), x + to_int(z == 4)
        first = y == 0
        r.from_behind = [
            pick(first, chip(near, zero + 6, z, zero), chip(x, y - 1, z, zero)),
            pick(first, chip(near, zero + 1, z, zero + 1), chip(x, y - 1, z, zero + 1)),
            pick(first, chip(far, zero + 7, z - 1, zero), chip(x, y - 1, z, zero)),
            pick(first, chip(far, zero + 7, z, zero + 1), chip(x, y - 1, z, zero + 1)),
        ]
        r.partners = 3 + to_int(r.relays) + to_int(r.lead)


def split(value):
    high = value.astype(BF16)
    return high, (value - high.astype(F32)).astype(BF16)


def product(a, b, dims):
    (ah, al), (bh, bl) = a, b
    dot = functools.partial(lax.dot_general, dimension_numbers=(dims, ((), ())), preferred_element_type=F32)
    return dot(ah, bh) + (dot(ah, bl) + dot(al, bh))


NT, NN = ((1,), (1,)), ((1,), (0,))


def unit_rows(source, target_high, target_low, rows, at, inverse=None):
    @pl.loop(0, rows // GROUP)
    def _(n):
        part = pl.ds(pl.multiple_of(n * GROUP, GROUP), GROUP)
        goal = pl.ds(pl.multiple_of(at + n * GROUP, GROUP), GROUP)
        value = source[part, :]
        inv = lax.rsqrt(jnp.sum(value * value, axis=-1, keepdims=True) + 1e-06)
        target_high[goal, :], target_low[goal, :] = split(value * inv)
        if inverse is not None:
            inverse[part, :] = jnp.broadcast_to(inv, (GROUP, 128))


def kernel(
    temp, bias, index, image, text, loss_out, image_out, text_out,
    held, own, inv, own_high, own_low, far_high, far_low, gates, total, loss, send_sem, recv_sem, load_sem,
):
    place = coordinates()
    routes = [Routes(mirrored(place, side)) for side in (0, 1)]
    sent = (text, image)

    def address(side, target):
        return device(*mirrored(target, side))

    barrier = pltpu.get_barrier_semaphore()
    for side, r in enumerate(routes):

        def greet(target, side=side):
            pl.semaphore_signal(barrier, inc=1, device_id=address(side, target), device_id_type=MESH)

        greet(r.from_cross)
        pl.when(r.relays)(lambda: greet(r.from_relay))

        @pl.when(r.lead)
        def _():
            for target in r.from_behind:
                greet(target)

        pl.when(r.follow)(lambda: greet(r.sibling))
    pl.semaphore_wait(barrier, routes[0].partners + routes[1].partners)

    def rows(i):
        return pl.ds(pl.multiple_of(i * CH, CH), CH)

    def slot(side, b, i):
        return held.at[side, b, rows(i)]

    def copy(kind, side, i):
        r = routes[side]
        source, goal, target = {
            CROSSING: (None, CROSS, r.to_cross),
            NEXT: (None, r.next_slot, r.to_next),
            ONWARD: (CROSS, r.onward_slot, r.to_onward),
            RELAYED: (RELAY, r.relayed_slot, r.to_relayed),
            SIB_OWN: (None, NEAR1, r.sibling),
            SIB_CROSS: (CROSS, FAR1, r.sibling),
            SIB_NEAR: (NEAR1, NEAR2, r.sibling),
            SIB_FAR: (FAR1, FAR2, r.sibling),
        }[kind]
        return pltpu.make_async_remote_copy(
            src_ref=sent[side].at[rows(i)] if source is None else slot(side, source, i),
            dst_ref=slot(side, goal, i),
            send_sem=send_sem.at[side, kind, i],
            recv_sem=recv_sem.at[side, goal, i],
            device_id=address(side, target),
            device_id_type=MESH,
        )

    def guarded(kind, side, act):
        r = routes[side]
        if kind in (CROSSING, NEXT, ONWARD):
            act()
        else:
            pl.when(r.relays if kind == RELAYED else r.lead)(act)

    def start(kind, side, i):
        guarded(kind, side, lambda: copy(kind, side, i).start())

    def arrived(side, b, i):
        pltpu.make_async_remote_copy(
            src_ref=slot(side, b, i),
            dst_ref=slot(side, b, i),
            send_sem=send_sem.at[side, 0, i],
            recv_sem=recv_sem.at[side, b, i],
            device_id=address(side, routes[side].sibling),
            device_id_type=MESH,
        ).wait_recv()

    @pl.loop(0, CHUNKS)
    def _(i):
        for side in (0, 1):
            start(CROSSING, side, i)
        for side in (0, 1):
            start(NEXT, side, i)
            start(SIB_OWN, side, i)

    loads = [pltpu.make_async_copy(sent[side], own.at[side], load_sem.at[side]) for side in (0, 1)]
    for load in loads:
        load.start()
    for side in (0, 1):
        loads[side].wait()
        unit_rows(own.at[side], own_high.at[side], own_low.at[side], ROWS, 0, inv.at[side])

    scale, shift = temp[0], bias[0]

    def halves(side):
        return own_high[side], own_low[side]

    score = scale * product(halves(0), halves(1), NT) + shift
    fade = jnp.exp(-jnp.abs(score))
    match = (lax.broadcasted_iota(jnp.int32, (ROWS, ROWS), 0) == index[...]).astype(F32)
    loss[...] = jnp.sum(jnp.maximum(score, 0.0) + jnp.log1p(fade) - match * score, axis=0, keepdims=True)
    gate = jnp.where(score >= 0, 1.0, fade) / (1.0 + fade) - match
    total[0] = product(split(gate.T), halves(0), NN)
    total[1] = product(split(gate), halves(1), NN)

    def score_chunk(side, b, i):
        at = LANES[b] * CH
        unit_rows(slot(side, b, i), far_high.at[side], far_low.at[side], CH, at)
        here = pl.ds(at, CH)
        score = scale * product((far_high[side, here], far_low[side, here]), halves(1 - side), NT) + shift
        fade = jnp.exp(-jnp.abs(score))
        if side == 0:
            loss[...] += jnp.sum(jnp.maximum(score, 0.0) + jnp.log1p(fade), axis=0, keepdims=True)
        gates[side, here] = jnp.where(score >= 0, 1.0, fade) / (1.0 + fade)

    @pl.loop(0, CHUNKS + 1)
    def _(i):
        @pl.when(i < CHUNKS)
        def _():
            for side, r in enumerate(routes):

                @pl.when(r.relays_near)
                def _():
                    arrived(side, RELAY, i)
                    copy(RELAYED, side, i).start()

            for side in (0, 1):
                arrived(side, CROSS, i)
                start(ONWARD, side, i)
                start(SIB_CROSS, side, i)
            for side, r in enumerate(routes):

                @pl.when(r.relays_far)
                def _():
                    arrived(side, RELAY, i)
                    copy(RELAYED, side, i).start()

        @pl.when(i > 0)
        def _():
            j = i - 1
            for side in (0, 1):
                arrived(side, NEAR1, j)
                start(SIB_NEAR, side, j)
            for side in (0, 1):
                score_chunk(side, CROSS, j)
                score_chunk(side, NEAR1, j)
            for side in (0, 1):
                arrived(side, NEAR2, j)
                score_chunk(side, NEAR2, j)
            for side in (0, 1):
                arrived(side, FAR1, j)
                start(SIB_FAR, side, j)
            for side in (0, 1):
                score_chunk(side, FAR1, j)
            for side in (0, 1):
                arrived(side, FAR2, j)
                score_chunk(side, FAR2, j)
            for side in (0, 1):
                total[side] += product(split(gates[side].T), (far_high[side], far_low[side]), NN)

    loss_out[...] = loss[...] / COUPLES_PER_ROW
    for side, out in ((0, image_out), (1, text_out)):
        mine = 1 - side

        @pl.loop(0, ROWS // GROUP)
        def _(n):
            part = pl.ds(pl.multiple_of(n * GROUP, GROUP), GROUP)
            inverse = inv[mine, part, :1]
            unit = own[mine, part, :] * inverse
            slope = scale * total[side, part, :]
            along = jnp.sum(unit * slope, axis=-1, keepdims=True)
            out[part, :] = inverse * (slope - unit * along)

    @pl.loop(0, CHUNKS)
    def _(i):
        for side in (0, 1):
            for kind in range(8):
                guarded(kind, side, lambda: copy(kind, side, i).wait_send())


def per_device(image, text, index, temp, bias):
    vmem, smem, anywhere = (pl.BlockSpec(memory_space=m) for m in (pltpu.VMEM, pltpu.SMEM, pl.ANY))
    block = jax.ShapeDtypeStruct((ROWS, WIDTH), F32)
    loss, image_slope, text_slope = pl.pallas_call(
        kernel,
        out_shape=(jax.ShapeDtypeStruct((1, ROWS), F32), block, block),
        in_specs=[smem, smem, vmem, anywhere, anywhere],
        out_specs=(vmem, vmem, vmem),
        scratch_shapes=[
            pltpu.VMEM((2, 6, ROWS, WIDTH), F32),
            pltpu.VMEM((2, ROWS, WIDTH), F32),
            pltpu.VMEM((2, ROWS, 128), F32),
            pltpu.VMEM((2, ROWS, WIDTH), BF16),
            pltpu.VMEM((2, ROWS, WIDTH), BF16),
            pltpu.VMEM((2, 5 * CH, WIDTH), BF16),
            pltpu.VMEM((2, 5 * CH, WIDTH), BF16),
            pltpu.VMEM((2, 5 * CH, ROWS), F32),
            pltpu.VMEM((2, ROWS, WIDTH), F32),
            pltpu.VMEM((1, ROWS), F32),
            pltpu.SemaphoreType.DMA((2, 8, CHUNKS)),
            pltpu.SemaphoreType.DMA((2, 6, CHUNKS)),
            pltpu.SemaphoreType.DMA((2,)),
        ],
        compiler_params=pltpu.CompilerParams(collective_id=0, has_side_effects=True, vmem_limit_bytes=56 * 2**20),
        name="pair_window",
    )(temp, bias, index, image, text)
    return loss.reshape(ROWS), image_slope, text_slope


def solution(mesh):
    rows = P(("blk", "hop"), None)
    return jax.shard_map(
        per_device,
        mesh=mesh,
        in_specs=(rows, rows, rows, P(), P()),
        out_specs=(P(("blk", "hop")), rows, rows),
        check_vma=False,
    )
```

```python
import functools

import jax
import jax.numpy as jnp
from jax import lax
from jax.experimental import pallas as pl
from jax.experimental.pallas import tpu as pltpu
from jax.sharding import PartitionSpec as P

COUPLES_PER_ROW = 1152
ROWS, WIDTH = 192, 1536
CHUNKS = 4
CH = ROWS // CHUNKS
GROUP = 16
PARTS = 4
MESH = pl.DeviceIdType.MESH
F32, BF16 = jnp.float32, jnp.bfloat16
CROSS, RELAY, NEAR1, NEAR2, FAR1, FAR2 = range(6)
SLOTS = (CROSS, NEAR1, NEAR2, FAR1, FAR2)
LANES = {CROSS: 0, NEAR1: 1, NEAR2: 2, FAR1: 3, FAR2: 4}
CROSSING, NEXT, ONWARD, RELAYED, SIB_OWN, SIB_CROSS, SIB_NEAR, SIB_FAR = range(8)


def to_int(p):
    return p.astype(jnp.int32)


def pick(p, a, b):
    return tuple(jnp.where(p, u, v) for u, v in zip(a, b))


def chip(x, y, z, c):
    return ((x + 8) % 4, (y + 8) % 8, (z + 16) % 8, c)


def coordinates():
    b, h = lax.axis_index("blk"), lax.axis_index("hop")
    return h // 2, (b // 2) % 8, (h % 2) * 4 + b // 16, b % 2


def device(x, y, z, c):
    return ((z % 4) * 16 + y * 2 + c, x * 2 + z // 4)


def mirrored(place, side):
    x, y, z, c = place
    return place if side == 0 else (3 - x, 7 - y, 7 - z, 1 - c)


class Routes:
    def __init__(r, place):
        x, y, z, c = place
        zero = 0 * c
        r.place = place
        r.last = y == 7
        r.lead = c == 0
        r.follow = c == 1
        r.sibling = (x, y, z, 1 - c)
        r.to_cross = chip(x + z // 4, y, z + 4, c)
        r.next_slot = jnp.where(r.last, RELAY, NEAR2 - c)
        r.relays = y > 0
        r.relays_near = y > 3
        r.relayed_chunk = jnp.where(r.relays_near, y - 4, 3 - y)
        r.near_x, r.far_x = x + to_int(z == 0), x - to_int(z == 4)
        r.to_relayed = chip(jnp.where(r.relays_near, r.near_x, r.far_x), zero, z, zero)
        r.relayed_slot = jnp.where(r.relays_near, NEAR2, FAR2) - c
        r.from_cross = chip(x - ((z + 4) % 8) // 4, y, z + 4, c)
        r.from_relay = chip(x, zero + 7, z - 1, c)
        r.partners = 3 + 6 * to_int(r.last) + to_int(r.relays) + to_int(r.lead)

    def to_next(r, i):
        x, y, z, c = r.place
        return pick(r.last, chip(x, 4 + i + 0 * c, z + 1, c), chip(x, y + 1, z, 0 * c))

    def to_onward(r, i):
        x, y, z, c = r.place
        direct = i == CHUNKS - 1
        at_end = chip(jnp.where(direct, x - to_int(z == 3), x), 3 - i + 0 * c, z + 1, jnp.where(direct, 0, c))
        return pick(r.last, at_end, chip(x, y + 1, z, 0 * c))

    def onward_slot(r, i):
        return jnp.where(r.last & (i < CHUNKS - 1), RELAY, FAR2 - r.place[3])

    def from_behind(r):
        x, y, z, c = r.place
        near, far = x - to_int(z == 0), x + to_int(z == 4)
        zero = 0 * c
        return [chip(near, zero + 7 - i, z, zero + core) for i in range(4) for core in (0, 1)] + [
            chip(far, zero + (3 - i if i < 3 else 7), z if i < 3 else z - 1, zero + core) for i in range(4) for core in (0, 1)
        ]


def split(value):
    high = value.astype(BF16)
    return high, (value - high.astype(F32)).astype(BF16)


def product(a, b, dims):
    (ah, al), (bh, bl) = a, b
    dot = functools.partial(lax.dot_general, dimension_numbers=(dims, ((), ())), preferred_element_type=F32)
    return dot(ah, bh) + (dot(ah, bl) + dot(al, bh))


NT, NN = ((1,), (1,)), ((1,), (0,))


def unit_rows(source, target_high, target_low):
    @pl.loop(0, ROWS // GROUP)
    def _(n):
        part = pl.ds(pl.multiple_of(n * GROUP, GROUP), GROUP)
        value = source[part, :]
        inv = lax.rsqrt(jnp.sum(value * value, axis=-1, keepdims=True) + 1e-06)
        target_high[part, :], target_low[part, :] = split(value * inv)


def slopes(temp, loss, image_sum, text_sum, image, text, loss_out, image_out, text_out):
    loss_out[...] = loss[0] / COUPLES_PER_ROW
    for total, source, out in ((image_sum, image, image_out), (text_sum, text, text_out)):
        value = source[...]
        inverse = lax.rsqrt(jnp.sum(value * value, axis=-1, keepdims=True) + 1e-06)
        unit = value * inverse
        slope = temp[0] * total[...]
        along = jnp.sum(unit * slope, axis=-1, keepdims=True)
        out[...] = inverse * (slope - unit * along)


def kernel(
    temp, bias, index, image, text, loss, image_sum, text_sum,
    held, own, own_high, own_low, far_high, far_low, far_inv, gates, send_sem, recv_sem, load_sem,
):
    place = coordinates()
    routes = [Routes(mirrored(place, side)) for side in (0, 1)]
    sent = (text, image)

    def address(side, target):
        return device(*mirrored(target, side))

    barrier = pltpu.get_barrier_semaphore()
    for side, r in enumerate(routes):

        def greet(target, side=side):
            pl.semaphore_signal(barrier, inc=1, device_id=address(side, target), device_id_type=MESH)

        greet(r.from_cross)
        pl.when(r.relays)(lambda: greet(r.from_relay))

        @pl.when(r.lead)
        def _():
            x, y, z, c = r.place

            @pl.when(y == 0)
            def _():
                for target in r.from_behind():
                    greet(target)

            @pl.when(y > 0)
            def _():
                for core in (0, 1):
                    for _ in (NEXT, ONWARD):
                        greet(chip(x, y - 1, z, 0 * c + core))

        pl.when(r.follow)(lambda: greet(r.sibling))
    pl.semaphore_wait(barrier, routes[0].partners + routes[1].partners)

    def rows(i):
        return pl.ds(pl.multiple_of(i * CH, CH), CH)

    def slot(side, b, i):
        return held.at[side, b, rows(i)]

    def copy(kind, side, i):
        r = routes[side]
        source, goal, target = {
            CROSSING: (None, CROSS, r.to_cross),
            NEXT: (None, r.next_slot, r.to_next(i)),
            ONWARD: (CROSS, r.onward_slot(i), r.to_onward(i)),
            RELAYED: (RELAY, r.relayed_slot, r.to_relayed),
            SIB_OWN: (None, NEAR1, r.sibling),
            SIB_CROSS: (CROSS, FAR1, r.sibling),
            SIB_NEAR: (NEAR1, NEAR2, r.sibling),
            SIB_FAR: (FAR1, FAR2, r.sibling),
        }[kind]
        return pltpu.make_async_remote_copy(
            src_ref=sent[side].at[rows(i)] if source is None else slot(side, source, i),
            dst_ref=slot(side, goal, i),
            send_sem=send_sem.at[side, kind, i],
            recv_sem=recv_sem.at[side, goal, i],
            device_id=address(side, target),
            device_id_type=MESH,
        )

    def guarded(kind, side, i, act):
        r = routes[side]
        if kind in (CROSSING, NEXT, ONWARD):
            act()
        elif kind == RELAYED:
            pl.when(r.relays & (r.relayed_chunk == i))(act)
        else:
            pl.when(r.lead)(act)

    def start(kind, side, i):
        guarded(kind, side, i, lambda: copy(kind, side, i).start())

    def arrived(side, b, i):
        pltpu.make_async_remote_copy(
            src_ref=slot(side, b, i),
            dst_ref=slot(side, b, i),
            send_sem=send_sem.at[side, 0, i],
            recv_sem=recv_sem.at[side, b, i],
            device_id=address(side, routes[side].sibling),
            device_id_type=MESH,
        ).wait_recv()

    @pl.loop(0, CHUNKS)
    def _(i):
        for side in (0, 1):
            start(CROSSING, side, i)
        for side in (0, 1):
            start(NEXT, side, i)
            start(SIB_OWN, side, i)

    loads = [pltpu.make_async_copy(sent[side], own.at[side], load_sem.at[side]) for side in (0, 1)]
    for load in loads:
        load.start()
    for side in (0, 1):
        loads[side].wait()
        unit_rows(own.at[side], own_high.at[side], own_low.at[side])

    scale, shift = temp[0], bias[0]

    def halves(side):
        return own_high[side], own_low[side]

    score = scale * product(halves(0), halves(1), NT) + shift
    fade = jnp.exp(-jnp.abs(score))
    match = (lax.broadcasted_iota(jnp.int32, (ROWS, ROWS), 0) == index[...]).astype(F32)
    loss[...] = jnp.sum(jnp.maximum(score, 0.0) + jnp.log1p(fade) - match * score, axis=0, keepdims=True)
    gate = jnp.where(score >= 0, 1.0, fade) / (1.0 + fade) - match
    image_sum[...] = product(split(gate.T), halves(0), NN)
    text_sum[...] = product(split(gate), halves(1), NN)

    def take(side, b, i):
        for n in range(CH // GROUP):
            part = pl.ds(pl.multiple_of(i * CH + n * GROUP, GROUP), GROUP)
            at = LANES[b] * CH + n * GROUP
            value = held[side, b, part, :]
            far_inv[side, pl.ds(at, GROUP)] = lax.rsqrt(jnp.sum(value * value, axis=-1, keepdims=True) + 1e-06)
            far_high[side, pl.ds(at, GROUP)], far_low[side, pl.ds(at, GROUP)] = split(value)

    def score_rows(side, first, count):
        here = pl.ds(first * CH, count * CH)
        inverse = far_inv[side, here]
        score = (scale * inverse) * product((far_high[side, here], far_low[side, here]), halves(1 - side), NT) + shift
        fade = jnp.exp(-jnp.abs(score))
        if side == 0:
            loss[...] += jnp.sum(jnp.maximum(score, 0.0) + jnp.log1p(fade), axis=0, keepdims=True)
        gates[side, here] = inverse * (jnp.where(score >= 0, 1.0, fade) / (1.0 + fade))

    @pl.loop(0, CHUNKS + 1)
    def _(i):
        @pl.when(i < CHUNKS)
        def _():
            for side, r in enumerate(routes):

                @pl.when(r.relays_near & (r.relayed_chunk == i))
                def _():
                    arrived(side, RELAY, i)
                    copy(RELAYED, side, i).start()

            for side in (0, 1):
                arrived(side, CROSS, i)
                start(ONWARD, side, i)
                start(SIB_CROSS, side, i)
            for side, r in enumerate(routes):

                @pl.when(r.relays & jnp.logical_not(r.relays_near) & (r.relayed_chunk == i))
                def _():
                    arrived(side, RELAY, i)
                    copy(RELAYED, side, i).start()

        @pl.when(i > 0)
        def _():
            j = i - 1

            def near_rows():
                for side in (0, 1):
                    arrived(side, NEAR2, j)
                    for b in (CROSS, NEAR1, NEAR2):
                        take(side, b, j)
                    score_rows(side, 0, 3)

            for side in (0, 1):
                arrived(side, NEAR1, j)
                start(SIB_NEAR, side, j)
            pl.when(i == CHUNKS)(near_rows)
            for side in (0, 1):
                arrived(side, FAR1, j)
                start(SIB_FAR, side, j)
            pl.when(i < CHUNKS)(near_rows)
            for side in (0, 1):
                arrived(side, FAR2, j)
                for b in (FAR1, FAR2):
                    take(side, b, j)
                score_rows(side, 3, 2)
            for side, total in ((0, image_sum), (1, text_sum)):
                total[...] += product(split(gates[side].T), (far_high[side], far_low[side]), NN)

    @pl.loop(0, CHUNKS)
    def _(i):
        for side in (0, 1):
            for kind in range(8):
                guarded(kind, side, i, lambda: copy(kind, side, i).wait_send())


def per_device(image, text, index, temp, bias):
    vmem, smem, anywhere = (pl.BlockSpec(memory_space=m) for m in (pltpu.VMEM, pltpu.SMEM, pl.ANY))
    block = jax.ShapeDtypeStruct((ROWS, WIDTH), F32)
    loss, image_sum, text_sum = pl.pallas_call(
        kernel,
        out_shape=(jax.ShapeDtypeStruct((1, ROWS), F32), block, block),
        in_specs=[smem, smem, vmem, anywhere, anywhere],
        out_specs=(vmem, vmem, vmem),
        scratch_shapes=[
            pltpu.VMEM((2, 6, ROWS, WIDTH), F32),
            pltpu.VMEM((2, ROWS, WIDTH), F32),
            pltpu.VMEM((2, ROWS, WIDTH), BF16),
            pltpu.VMEM((2, ROWS, WIDTH), BF16),
            pltpu.VMEM((2, 5 * CH, WIDTH), BF16),
            pltpu.VMEM((2, 5 * CH, WIDTH), BF16),
            pltpu.VMEM((2, 5 * CH, 1), F32),
            pltpu.VMEM((2, 5 * CH, ROWS), F32),
            pltpu.SemaphoreType.DMA((2, 8, CHUNKS)),
            pltpu.SemaphoreType.DMA((2, 6, CHUNKS)),
            pltpu.SemaphoreType.DMA((2,)),
        ],
        compiler_params=pltpu.CompilerParams(collective_id=0, has_side_effects=True, vmem_limit_bytes=56 * 2**20),
        name="pair_window",
    )(temp, bias, index, image, text)
    part = pl.BlockSpec((ROWS // PARTS, WIDTH), lambda n: (n, 0))
    return pl.pallas_call(
        slopes,
        grid=(PARTS,),
        out_shape=(jax.ShapeDtypeStruct((ROWS,), F32), block, block),
        in_specs=[smem, pl.BlockSpec((1, ROWS), lambda n: (0, 0)), part, part, part, part],
        out_specs=(pl.BlockSpec((ROWS,), lambda n: (0,)), part, part),
        name="row_slopes",
    )(temp, loss, image_sum, text_sum, image, text)


def solution(mesh):
    rows = P(("blk", "hop"), None)
    return jax.shard_map(
        per_device,
        mesh=mesh,
        in_specs=(rows, rows, rows, P(), P()),
        out_specs=(P(("blk", "hop")), rows, rows),
        check_vma=False,
    )
```

```python
import functools

import jax
import jax.numpy as jnp
from jax import lax
from jax.experimental import pallas as pl
from jax.experimental.pallas import tpu as pltpu
from jax.sharding import PartitionSpec as P

COUPLES_PER_ROW = 1152
ROWS, WIDTH = 192, 1536
CHUNKS = 4
CH = ROWS // CHUNKS
GROUP = 16
PARTS = 2
MESH = pl.DeviceIdType.MESH
F32, BF16 = jnp.float32, jnp.bfloat16
CROSS, RELAY, NEAR1, NEAR2, FAR1, FAR2 = range(6)
SLOTS = (CROSS, NEAR1, NEAR2, FAR1, FAR2)
LANES = {CROSS: 0, NEAR1: 1, NEAR2: 2, FAR1: 3, FAR2: 4}
CROSSING, NEXT, ONWARD, RELAYED, SIB_OWN, SIB_CROSS, SIB_NEAR, SIB_FAR = range(8)


def to_int(p):
    return p.astype(jnp.int32)


def pick(p, a, b):
    return tuple(jnp.where(p, u, v) for u, v in zip(a, b))


def chip(x, y, z, c):
    return ((x + 8) % 4, (y + 8) % 8, (z + 16) % 8, c)


def coordinates():
    b, h = lax.axis_index("blk"), lax.axis_index("hop")
    return h // 2, (b // 2) % 8, (h % 2) * 4 + b // 16, b % 2


def device(x, y, z, c):
    return ((z % 4) * 16 + y * 2 + c, x * 2 + z // 4)


def mirrored(place, side):
    x, y, z, c = place
    return place if side == 0 else (3 - x, 7 - y, 7 - z, 1 - c)


class Routes:
    def __init__(r, place):
        x, y, z, c = place
        zero = 0 * c
        r.place = place
        r.last = y == 7
        r.lead = c == 0
        r.follow = c == 1
        r.sibling = (x, y, z, 1 - c)
        r.to_cross = chip(x + z // 4, y, z + 4, c)
        r.next_slot = jnp.where(r.last, RELAY, NEAR2 - c)
        r.relays = y > 0
        r.relays_near = y > 3
        r.relayed_chunk = jnp.where(r.relays_near, y - 4, 3 - y)
        r.near_x, r.far_x = x + to_int(z == 0), x - to_int(z == 4)
        r.to_relayed = chip(jnp.where(r.relays_near, r.near_x, r.far_x), zero, z, zero)
        r.relayed_slot = jnp.where(r.relays_near, NEAR2, FAR2) - c
        r.from_cross = chip(x - ((z + 4) % 8) // 4, y, z + 4, c)
        r.from_relay = chip(x, zero + 7, z - 1, c)
        r.partners = 3 + 6 * to_int(r.last) + to_int(r.relays) + to_int(r.lead)

    def to_next(r, i):
        x, y, z, c = r.place
        return pick(r.last, chip(x, 4 + i + 0 * c, z + 1, c), chip(x, y + 1, z, 0 * c))

    def to_onward(r, i):
        x, y, z, c = r.place
        direct = i == CHUNKS - 1
        at_end = chip(jnp.where(direct, x - to_int(z == 3), x), 3 - i + 0 * c, z + 1, jnp.where(direct, 0, c))
        return pick(r.last, at_end, chip(x, y + 1, z, 0 * c))

    def onward_slot(r, i):
        return jnp.where(r.last & (i < CHUNKS - 1), RELAY, FAR2 - r.place[3])

    def from_behind(r):
        x, y, z, c = r.place
        near, far = x - to_int(z == 0), x + to_int(z == 4)
        zero = 0 * c
        return [chip(near, zero + 7 - i, z, zero + core) for i in range(4) for core in (0, 1)] + [
            chip(far, zero + (3 - i if i < 3 else 7), z if i < 3 else z - 1, zero + core) for i in range(4) for core in (0, 1)
        ]


def split(value):
    high = value.astype(BF16)
    return high, (value - high.astype(F32)).astype(BF16)


def product(a, b, dims):
    (ah, al), (bh, bl) = a, b
    dot = functools.partial(lax.dot_general, dimension_numbers=(dims, ((), ())), preferred_element_type=F32)
    return dot(ah, bh) + (dot(ah, bl) + dot(al, bh))


NT, NN = ((1,), (1,)), ((1,), (0,))


def unit_rows(source, target_high, target_low):
    @pl.loop(0, ROWS // GROUP)
    def _(n):
        part = pl.ds(pl.multiple_of(n * GROUP, GROUP), GROUP)
        value = source[part, :]
        inv = lax.rsqrt(jnp.sum(value * value, axis=-1, keepdims=True) + 1e-06)
        target_high[part, :], target_low[part, :] = split(value * inv)


def slopes(temp, loss, image_sum, text_sum, image, text, loss_out, image_out, text_out):
    loss_out[...] = loss[0] / COUPLES_PER_ROW
    for total, source, out in ((image_sum, image, image_out), (text_sum, text, text_out)):
        value = source[...]
        inverse = lax.rsqrt(jnp.sum(value * value, axis=-1, keepdims=True) + 1e-06)
        unit = value * inverse
        slope = temp[0] * total[...]
        along = jnp.sum(unit * slope, axis=-1, keepdims=True)
        out[...] = inverse * (slope - unit * along)


def kernel(
    temp, bias, index, image, text, loss, image_sum, text_sum,
    held, own, own_high, own_low, far_high, far_low, far_inv, gates, send_sem, recv_sem, load_sem,
):
    place = coordinates()
    routes = [Routes(mirrored(place, side)) for side in (0, 1)]
    sent = (text, image)

    def address(side, target):
        return device(*mirrored(target, side))

    barrier = pltpu.get_barrier_semaphore()
    for side, r in enumerate(routes):

        def greet(target, side=side):
            pl.semaphore_signal(barrier, inc=1, device_id=address(side, target), device_id_type=MESH)

        greet(r.from_cross)
        pl.when(r.relays)(lambda: greet(r.from_relay))

        @pl.when(r.lead)
        def _():
            x, y, z, c = r.place

            @pl.when(y == 0)
            def _():
                for target in r.from_behind():
                    greet(target)

            @pl.when(y > 0)
            def _():
                for core in (0, 1):
                    for _ in (NEXT, ONWARD):
                        greet(chip(x, y - 1, z, 0 * c + core))

        pl.when(r.follow)(lambda: greet(r.sibling))
    pl.semaphore_wait(barrier, routes[0].partners + routes[1].partners)

    def rows(i):
        return pl.ds(pl.multiple_of(i * CH, CH), CH)

    def slot(side, b, i):
        return held.at[side, b, rows(i)]

    def copy(kind, side, i):
        r = routes[side]
        source, goal, target = {
            CROSSING: (None, CROSS, r.to_cross),
            NEXT: (None, r.next_slot, r.to_next(i)),
            ONWARD: (CROSS, r.onward_slot(i), r.to_onward(i)),
            RELAYED: (RELAY, r.relayed_slot, r.to_relayed),
            SIB_OWN: (None, NEAR1, r.sibling),
            SIB_CROSS: (CROSS, FAR1, r.sibling),
            SIB_NEAR: (NEAR1, NEAR2, r.sibling),
            SIB_FAR: (FAR1, FAR2, r.sibling),
        }[kind]
        return pltpu.make_async_remote_copy(
            src_ref=sent[side].at[rows(i)] if source is None else slot(side, source, i),
            dst_ref=slot(side, goal, i),
            send_sem=send_sem.at[side, kind, i],
            recv_sem=recv_sem.at[side, goal, i],
            device_id=address(side, target),
            device_id_type=MESH,
        )

    def guarded(kind, side, i, act):
        r = routes[side]
        if kind in (CROSSING, NEXT, ONWARD):
            act()
        elif kind == RELAYED:
            pl.when(r.relays & (r.relayed_chunk == i))(act)
        else:
            pl.when(r.lead)(act)

    def start(kind, side, i):
        guarded(kind, side, i, lambda: copy(kind, side, i).start())

    def arrived(side, b, i):
        pltpu.make_async_remote_copy(
            src_ref=slot(side, b, i),
            dst_ref=slot(side, b, i),
            send_sem=send_sem.at[side, 0, i],
            recv_sem=recv_sem.at[side, b, i],
            device_id=address(side, routes[side].sibling),
            device_id_type=MESH,
        ).wait_recv()

    @pl.loop(0, CHUNKS)
    def _(i):
        @pl.when(i < 2)
        def _():
            for side in (0, 1):
                start(CROSSING, side, i)

        for side in (0, 1):
            start(NEXT, side, i)
            start(SIB_OWN, side, i)

    loads = [pltpu.make_async_copy(sent[side], own.at[side], load_sem.at[side]) for side in (0, 1)]
    for load in loads:
        load.start()

    scale, shift = temp[0], bias[0]

    def halves(side):
        return own_high[side], own_low[side]

    def own_pair():
        for side in (0, 1):
            loads[side].wait()
            unit_rows(own.at[side], own_high.at[side], own_low.at[side])

        score = scale * product(halves(0), halves(1), NT) + shift
        fade = jnp.exp(-jnp.abs(score))
        match = (lax.broadcasted_iota(jnp.int32, (ROWS, ROWS), 0) == index[...]).astype(F32)
        loss[...] = jnp.sum(jnp.maximum(score, 0.0) + jnp.log1p(fade) - match * score, axis=0, keepdims=True)
        gate = jnp.where(score >= 0, 1.0, fade) / (1.0 + fade) - match
        image_sum[...] = product(split(gate.T), halves(0), NN)
        text_sum[...] = product(split(gate), halves(1), NN)

    def take(side, b, i):
        for n in range(CH // GROUP):
            part = pl.ds(pl.multiple_of(i * CH + n * GROUP, GROUP), GROUP)
            at = LANES[b] * CH + n * GROUP
            value = held[side, b, part, :]
            far_inv[side, pl.ds(at, GROUP)] = lax.rsqrt(jnp.sum(value * value, axis=-1, keepdims=True) + 1e-06)
            far_high[side, pl.ds(at, GROUP)], far_low[side, pl.ds(at, GROUP)] = split(value)

    def score_rows(side, first, count):
        here = pl.ds(first * CH, count * CH)
        inverse = far_inv[side, here]
        score = (scale * inverse) * product((far_high[side, here], far_low[side, here]), halves(1 - side), NT) + shift
        fade = jnp.exp(-jnp.abs(score))
        if side == 0:
            loss[...] += jnp.sum(jnp.maximum(score, 0.0) + jnp.log1p(fade), axis=0, keepdims=True)
        gates[side, here] = inverse * (jnp.where(score >= 0, 1.0, fade) / (1.0 + fade))

    @pl.loop(0, CHUNKS + 1)
    def _(i):
        @pl.when(i < CHUNKS)
        def _():
            for side, r in enumerate(routes):

                @pl.when(r.relays_near & (r.relayed_chunk == i))
                def _():
                    arrived(side, RELAY, i)
                    copy(RELAYED, side, i).start()

            for side in (0, 1):
                arrived(side, CROSS, i)
                start(ONWARD, side, i)
                start(SIB_CROSS, side, i)

            @pl.when(i + 2 < CHUNKS)
            def _():
                for side in (0, 1):
                    start(CROSSING, side, i + 2)

            for side, r in enumerate(routes):

                @pl.when(r.relays & jnp.logical_not(r.relays_near) & (r.relayed_chunk == i))
                def _():
                    arrived(side, RELAY, i)
                    copy(RELAYED, side, i).start()

        pl.when(i == 0)(own_pair)

        @pl.when(i > 0)
        def _():
            j = i - 1

            def near_rows():
                for side in (0, 1):
                    arrived(side, NEAR2, j)
                    for b in (CROSS, NEAR1, NEAR2):
                        take(side, b, j)
                    score_rows(side, 0, 3)

            for side in (0, 1):
                arrived(side, NEAR1, j)
                start(SIB_NEAR, side, j)
            pl.when(i == CHUNKS)(near_rows)
            for side in (0, 1):
                arrived(side, FAR1, j)
                start(SIB_FAR, side, j)
            pl.when(i < CHUNKS)(near_rows)
            for side in (0, 1):
                arrived(side, FAR2, j)
                for b in (FAR1, FAR2):
                    take(side, b, j)
                score_rows(side, 3, 2)
            for side, total in ((0, image_sum), (1, text_sum)):
                total[...] += product(split(gates[side].T), (far_high[side], far_low[side]), NN)

    @pl.loop(0, CHUNKS)
    def _(i):
        for side in (0, 1):
            for kind in range(8):
                guarded(kind, side, i, lambda: copy(kind, side, i).wait_send())


def per_device(image, text, index, temp, bias):
    vmem, smem, anywhere = (pl.BlockSpec(memory_space=m) for m in (pltpu.VMEM, pltpu.SMEM, pl.ANY))
    block = jax.ShapeDtypeStruct((ROWS, WIDTH), F32)
    loss, image_sum, text_sum = pl.pallas_call(
        kernel,
        out_shape=(jax.ShapeDtypeStruct((1, ROWS), F32), block, block),
        in_specs=[smem, smem, vmem, anywhere, anywhere],
        out_specs=(vmem, vmem, vmem),
        scratch_shapes=[
            pltpu.VMEM((2, 6, ROWS, WIDTH), F32),
            pltpu.VMEM((2, ROWS, WIDTH), F32),
            pltpu.VMEM((2, ROWS, WIDTH), BF16),
            pltpu.VMEM((2, ROWS, WIDTH), BF16),
            pltpu.VMEM((2, 5 * CH, WIDTH), BF16),
            pltpu.VMEM((2, 5 * CH, WIDTH), BF16),
            pltpu.VMEM((2, 5 * CH, 1), F32),
            pltpu.VMEM((2, 5 * CH, ROWS), F32),
            pltpu.SemaphoreType.DMA((2, 8, CHUNKS)),
            pltpu.SemaphoreType.DMA((2, 6, CHUNKS)),
            pltpu.SemaphoreType.DMA((2,)),
        ],
        compiler_params=pltpu.CompilerParams(collective_id=0, has_side_effects=True, vmem_limit_bytes=56 * 2**20),
        name="pair_window",
    )(temp, bias, index, image, text)
    part = pl.BlockSpec((ROWS // PARTS, WIDTH), lambda n: (n, 0))
    return pl.pallas_call(
        slopes,
        grid=(PARTS,),
        out_shape=(jax.ShapeDtypeStruct((ROWS,), F32), block, block),
        in_specs=[smem, pl.BlockSpec((1, ROWS), lambda n: (0, 0)), part, part, part, part],
        out_specs=(pl.BlockSpec((ROWS,), lambda n: (0,)), part, part),
        name="row_slopes",
    )(temp, loss, image_sum, text_sum, image, text)


def solution(mesh):
    rows = P(("blk", "hop"), None)
    return jax.shard_map(
        per_device,
        mesh=mesh,
        in_specs=(rows, rows, rows, P(), P()),
        out_specs=(P(("blk", "hop")), rows, rows),
        check_vma=False,
    )
```

```python
import functools

import jax
import jax.numpy as jnp
from jax import lax
from jax.experimental import pallas as pl
from jax.experimental.pallas import tpu as pltpu
from jax.sharding import PartitionSpec as P

COUPLES_PER_ROW = 1152
ROWS, WIDTH = 192, 1536
CHUNKS = 4
CH = ROWS // CHUNKS
GROUP = 16
PARTS = 1
MESH = pl.DeviceIdType.MESH
F32, BF16 = jnp.float32, jnp.bfloat16
CROSS, RELAY, NEAR1, NEAR2, FAR1, FAR2 = range(6)
SLOTS = (CROSS, NEAR1, NEAR2, FAR1, FAR2)
LANES = {CROSS: 0, NEAR1: 1, NEAR2: 2, FAR1: 3, FAR2: 4}
CROSSING, NEXT, ONWARD, RELAYED, SIB_OWN, SIB_CROSS, SIB_NEAR, SIB_FAR = range(8)


def to_int(p):
    return p.astype(jnp.int32)


def pick(p, a, b):
    return tuple(jnp.where(p, u, v) for u, v in zip(a, b))


def chip(x, y, z, c):
    return ((x + 8) % 4, (y + 8) % 8, (z + 16) % 8, c)


def coordinates():
    b, h = lax.axis_index("blk"), lax.axis_index("hop")
    return h // 2, (b // 2) % 8, (h % 2) * 4 + b // 16, b % 2


def device(x, y, z, c):
    return ((z % 4) * 16 + y * 2 + c, x * 2 + z // 4)


def mirrored(place, side):
    x, y, z, c = place
    return place if side == 0 else (3 - x, 7 - y, 7 - z, 1 - c)


class Routes:
    def __init__(r, place):
        x, y, z, c = place
        zero = 0 * c
        r.place = place
        r.last = y == 7
        r.lead = c == 0
        r.follow = c == 1
        r.sibling = (x, y, z, 1 - c)
        r.to_cross = chip(x + z // 4, y, z + 4, c)
        r.next_slot = jnp.where(r.last, RELAY, NEAR2 - c)
        r.relays = y > 0
        r.relays_near = y > 3
        r.relayed_chunk = jnp.where(r.relays_near, y - 4, 3 - y)
        r.near_x, r.far_x = x + to_int(z == 0), x - to_int(z == 4)
        r.to_relayed = chip(jnp.where(r.relays_near, r.near_x, r.far_x), zero, z, zero)
        r.relayed_slot = jnp.where(r.relays_near, NEAR2, FAR2) - c
        r.from_cross = chip(x - ((z + 4) % 8) // 4, y, z + 4, c)
        r.from_relay = chip(x, zero + 7, z - 1, c)
        r.partners = 3 + 6 * to_int(r.last) + to_int(r.relays) + to_int(r.lead)

    def to_next(r, i):
        x, y, z, c = r.place
        return pick(r.last, chip(x, 4 + i + 0 * c, z + 1, c), chip(x, y + 1, z, 0 * c))

    def to_onward(r, i):
        x, y, z, c = r.place
        direct = i == CHUNKS - 1
        at_end = chip(jnp.where(direct, x - to_int(z == 3), x), 3 - i + 0 * c, z + 1, jnp.where(direct, 0, c))
        return pick(r.last, at_end, chip(x, y + 1, z, 0 * c))

    def onward_slot(r, i):
        return jnp.where(r.last & (i < CHUNKS - 1), RELAY, FAR2 - r.place[3])

    def from_behind(r):
        x, y, z, c = r.place
        near, far = x - to_int(z == 0), x + to_int(z == 4)
        zero = 0 * c
        return [chip(near, zero + 7 - i, z, zero + core) for i in range(4) for core in (0, 1)] + [
            chip(far, zero + (3 - i if i < 3 else 7), z if i < 3 else z - 1, zero + core) for i in range(4) for core in (0, 1)
        ]


def split(value):
    high = value.astype(BF16)
    return high, (value - high.astype(F32)).astype(BF16)


def product(a, b, dims):
    (ah, al), (bh, bl) = a, b
    dot = functools.partial(lax.dot_general, dimension_numbers=(dims, ((), ())), preferred_element_type=F32)
    return dot(ah, bh) + (dot(ah, bl) + dot(al, bh))


NT, NN = ((1,), (1,)), ((1,), (0,))


def unit_rows(source, target_high, target_low):
    @pl.loop(0, ROWS // GROUP)
    def _(n):
        part = pl.ds(pl.multiple_of(n * GROUP, GROUP), GROUP)
        value = source[part, :]
        inv = lax.rsqrt(jnp.sum(value * value, axis=-1, keepdims=True) + 1e-06)
        target_high[part, :], target_low[part, :] = split(value * inv)


def slopes(temp, loss, image_sum, text_sum, image, text, loss_out, image_out, text_out):
    loss_out[...] = loss[0] / COUPLES_PER_ROW
    for total, source, out in ((image_sum, image, image_out), (text_sum, text, text_out)):
        value = source[...]
        inverse = lax.rsqrt(jnp.sum(value * value, axis=-1, keepdims=True) + 1e-06)
        unit = value * inverse
        slope = temp[0] * total[...]
        along = jnp.sum(unit * slope, axis=-1, keepdims=True)
        out[...] = inverse * (slope - unit * along)


def kernel(
    temp, bias, index, image, text, loss, image_sum, text_sum,
    held, own, own_high, own_low, far_high, far_low, far_inv, gates, send_sem, recv_sem, load_sem,
):
    place = coordinates()
    routes = [Routes(mirrored(place, side)) for side in (0, 1)]
    sent = (text, image)

    def address(side, target):
        return device(*mirrored(target, side))

    barrier = pltpu.get_barrier_semaphore()
    for side, r in enumerate(routes):

        def greet(target, side=side):
            pl.semaphore_signal(barrier, inc=1, device_id=address(side, target), device_id_type=MESH)

        greet(r.from_cross)
        pl.when(r.relays)(lambda: greet(r.from_relay))

        @pl.when(r.lead)
        def _():
            x, y, z, c = r.place

            @pl.when(y == 0)
            def _():
                for target in r.from_behind():
                    greet(target)

            @pl.when(y > 0)
            def _():
                for core in (0, 1):
                    for _ in (NEXT, ONWARD):
                        greet(chip(x, y - 1, z, 0 * c + core))

        pl.when(r.follow)(lambda: greet(r.sibling))
    pl.semaphore_wait(barrier, routes[0].partners + routes[1].partners)

    def rows(i):
        return pl.ds(pl.multiple_of(i * CH, CH), CH)

    def slot(side, b, i):
        return held.at[side, b, rows(i)]

    def copy(kind, side, i):
        r = routes[side]
        source, goal, target = {
            CROSSING: (None, CROSS, r.to_cross),
            NEXT: (None, r.next_slot, r.to_next(i)),
            ONWARD: (CROSS, r.onward_slot(i), r.to_onward(i)),
            RELAYED: (RELAY, r.relayed_slot, r.to_relayed),
            SIB_OWN: (None, NEAR1, r.sibling),
            SIB_CROSS: (CROSS, FAR1, r.sibling),
            SIB_NEAR: (NEAR1, NEAR2, r.sibling),
            SIB_FAR: (FAR1, FAR2, r.sibling),
        }[kind]
        return pltpu.make_async_remote_copy(
            src_ref=sent[side].at[rows(i)] if source is None else slot(side, source, i),
            dst_ref=slot(side, goal, i),
            send_sem=send_sem.at[side, kind, i],
            recv_sem=recv_sem.at[side, goal, i],
            device_id=address(side, target),
            device_id_type=MESH,
        )

    def guarded(kind, side, i, act):
        r = routes[side]
        if kind in (CROSSING, NEXT, ONWARD):
            act()
        elif kind == RELAYED:
            pl.when(r.relays & (r.relayed_chunk == i))(act)
        else:
            pl.when(r.lead)(act)

    def start(kind, side, i):
        guarded(kind, side, i, lambda: copy(kind, side, i).start())

    def arrived(side, b, i):
        pltpu.make_async_remote_copy(
            src_ref=slot(side, b, i),
            dst_ref=slot(side, b, i),
            send_sem=send_sem.at[side, 0, i],
            recv_sem=recv_sem.at[side, b, i],
            device_id=address(side, routes[side].sibling),
            device_id_type=MESH,
        ).wait_recv()

    @pl.loop(0, CHUNKS)
    def _(i):
        @pl.when(i < 2)
        def _():
            for side in (0, 1):
                start(CROSSING, side, i)

        for side in (0, 1):
            start(NEXT, side, i)
            start(SIB_OWN, side, i)

    loads = [pltpu.make_async_copy(sent[side], own.at[side], load_sem.at[side]) for side in (0, 1)]
    for load in loads:
        load.start()

    scale, shift = temp[0], bias[0]

    def halves(side):
        return own_high[side], own_low[side]

    def own_pair():
        for side in (0, 1):
            loads[side].wait()
            unit_rows(own.at[side], own_high.at[side], own_low.at[side])

        score = scale * product(halves(0), halves(1), NT) + shift
        fade = jnp.exp(-jnp.abs(score))
        match = (lax.broadcasted_iota(jnp.int32, (ROWS, ROWS), 0) == index[...]).astype(F32)
        loss[...] = jnp.sum(jnp.maximum(score, 0.0) + jnp.log1p(fade) - match * score, axis=0, keepdims=True)
        gate = jnp.where(score >= 0, 1.0, fade) / (1.0 + fade) - match
        image_sum[...] = product(split(gate.T), halves(0), NN)
        text_sum[...] = product(split(gate), halves(1), NN)

    def take(side, b, i):
        for n in range(CH // GROUP):
            part = pl.ds(pl.multiple_of(i * CH + n * GROUP, GROUP), GROUP)
            at = LANES[b] * CH + n * GROUP
            value = held[side, b, part, :]
            far_inv[side, pl.ds(at, GROUP)] = lax.rsqrt(jnp.sum(value * value, axis=-1, keepdims=True) + 1e-06)
            far_high[side, pl.ds(at, GROUP)], far_low[side, pl.ds(at, GROUP)] = split(value)

    def score_rows(side, first, count):
        here = pl.ds(first * CH, count * CH)
        inverse = far_inv[side, here]
        score = (scale * inverse) * product((far_high[side, here], far_low[side, here]), halves(1 - side), NT) + shift
        fade = jnp.exp(-jnp.abs(score))
        if side == 0:
            loss[...] += jnp.sum(jnp.maximum(score, 0.0) + jnp.log1p(fade), axis=0, keepdims=True)
        gates[side, here] = inverse * (jnp.where(score >= 0, 1.0, fade) / (1.0 + fade))

    @pl.loop(0, CHUNKS + 1)
    def _(i):
        @pl.when(i < CHUNKS)
        def _():
            for side, r in enumerate(routes):

                @pl.when(r.relays_near & (r.relayed_chunk == i))
                def _():
                    arrived(side, RELAY, i)
                    copy(RELAYED, side, i).start()

            for side in (0, 1):
                arrived(side, CROSS, i)
                start(ONWARD, side, i)
                start(SIB_CROSS, side, i)

            @pl.when(i + 2 < CHUNKS)
            def _():
                for side in (0, 1):
                    start(CROSSING, side, i + 2)

            for side, r in enumerate(routes):

                @pl.when(r.relays & jnp.logical_not(r.relays_near) & (r.relayed_chunk == i))
                def _():
                    arrived(side, RELAY, i)
                    copy(RELAYED, side, i).start()

        pl.when(i == 0)(own_pair)

        @pl.when(i > 0)
        def _():
            j = i - 1

            def near_rows():
                for side in (0, 1):
                    arrived(side, NEAR2, j)
                    for b in (CROSS, NEAR1, NEAR2):
                        take(side, b, j)
                    score_rows(side, 0, 3)

            for side in (0, 1):
                arrived(side, NEAR1, j)
                start(SIB_NEAR, side, j)
            pl.when(i == CHUNKS)(near_rows)
            for side in (0, 1):
                arrived(side, FAR1, j)
                start(SIB_FAR, side, j)
            pl.when(i < CHUNKS)(near_rows)
            for side in (0, 1):
                arrived(side, FAR2, j)
                for b in (FAR1, FAR2):
                    take(side, b, j)
                score_rows(side, 3, 2)
            for side, total in ((0, image_sum), (1, text_sum)):
                total[...] += product(split(gates[side].T), (far_high[side], far_low[side]), NN)

    @pl.loop(0, CHUNKS)
    def _(i):
        for side in (0, 1):
            for kind in range(8):
                guarded(kind, side, i, lambda: copy(kind, side, i).wait_send())


def per_device(image, text, index, temp, bias):
    vmem, smem, anywhere = (pl.BlockSpec(memory_space=m) for m in (pltpu.VMEM, pltpu.SMEM, pl.ANY))
    block = jax.ShapeDtypeStruct((ROWS, WIDTH), F32)
    loss, image_sum, text_sum = pl.pallas_call(
        kernel,
        out_shape=(jax.ShapeDtypeStruct((1, ROWS), F32), block, block),
        in_specs=[smem, smem, vmem, anywhere, anywhere],
        out_specs=(vmem, vmem, vmem),
        scratch_shapes=[
            pltpu.VMEM((2, 6, ROWS, WIDTH), F32),
            pltpu.VMEM((2, ROWS, WIDTH), F32),
            pltpu.VMEM((2, ROWS, WIDTH), BF16),
            pltpu.VMEM((2, ROWS, WIDTH), BF16),
            pltpu.VMEM((2, 5 * CH, WIDTH), BF16),
            pltpu.VMEM((2, 5 * CH, WIDTH), BF16),
            pltpu.VMEM((2, 5 * CH, 1), F32),
            pltpu.VMEM((2, 5 * CH, ROWS), F32),
            pltpu.SemaphoreType.DMA((2, 8, CHUNKS)),
            pltpu.SemaphoreType.DMA((2, 6, CHUNKS)),
            pltpu.SemaphoreType.DMA((2,)),
        ],
        compiler_params=pltpu.CompilerParams(collective_id=0, has_side_effects=True, vmem_limit_bytes=56 * 2**20),
        name="pair_window",
    )(temp, bias, index, image, text)
    part = pl.BlockSpec((ROWS // PARTS, WIDTH), lambda n: (n, 0))
    return pl.pallas_call(
        slopes,
        grid=(PARTS,),
        out_shape=(jax.ShapeDtypeStruct((ROWS,), F32), block, block),
        in_specs=[smem, pl.BlockSpec((1, ROWS), lambda n: (0, 0)), part, part, part, part],
        out_specs=(pl.BlockSpec((ROWS,), lambda n: (0,)), part, part),
        compiler_params=pltpu.CompilerParams(vmem_limit_bytes=32 * 2**20),
        name="row_slopes",
    )(temp, loss, image_sum, text_sum, image, text)


def solution(mesh):
    rows = P(("blk", "hop"), None)
    return jax.shard_map(
        per_device,
        mesh=mesh,
        in_specs=(rows, rows, rows, P(), P()),
        out_specs=(P(("blk", "hop")), rows, rows),
        check_vma=False,
    )
```
